32 devices in a mesh: row: 8 (over z, x), col: 4 (over y, core).
Axes of the slice: x: 2, y: 2, z: 4, core: 2. Of those that a mesh axis runs over, the one named last changes fastest.
Arguments:
- hidden: bfloat16 [8192, 1600], P('row', 'col'), may hold values from -60 to 60
- up_weight: bfloat16 [1600, 6400], P('row', 'col'), may hold values from -0.15625 to 0.15625
- up_bias: float32 [6400], P('col'), may hold values from -3 to 3
- down_weight: bfloat16 [6400, 1600], P('col', 'row'), may hold values from -0.078125 to 0.078125
- down_bias: float32 [1600], P('col'), may hold values from -3 to 3
- query_key_value_weight: bfloat16 [1600, 4800], P('row', 'col'), may hold values from -0.15625 to 0.15625
- query_key_value_bias: float32 [4800], P('col'), may hold values from -3 to 3
- block_norm_gain: float32 [1600], replicated, may hold values from 0.1 to 1.9
- block_norm_shift: float32 [1600], replicated, may hold values from -3 to 3
- following_norm_gain: float32 [1600], replicated, may hold values from 0.1 to 1.9
- following_norm_shift: float32 [1600], replicated, may hold values from -3 to 3
- up_down_factors: bfloat16 [32, 16, 1600], P('row'), may hold values from -0.15625 to 0.15625
- up_up_factors: bfloat16 [32, 16, 6400], P('row', None, 'col'), may hold values from -1.5 to 1.5
- query_key_value_down_factors: bfloat16 [32, 16, 1600], P('row'), may hold values from -0.15625 to 0.15625
- query_key_value_up_factors: bfloat16 [32, 16, 4800], P('row', None, 'col'), may hold values from -1.5 to 1.5
- adapter_storage_slot: int32 [32], replicated, may hold values from 0 to 31, as said below
- tile_adapter_index: int32 [64], P('row'), may hold values from 0 to 31, as said below
- tile_token_rows: int32 [64], P('row'), may hold values from 1 to 128, as said below
Outputs:
- h_out: bfloat16 [8192, 1600], P('row', 'col')
- qkv: bfloat16 [8192, 4800], P('row', 'col')
The draws below stay inside these ranges and needn't reach their ends.
Inputs may be any that keep to these rules, and one draw needn't show every extreme that they name: A permutation: adapter a is stored in slot adapter_storage_slot[a], and index r of row holds slots r * 4 to (r + 1) * 4 - 1. `tile_adapter_index`: the 8 tiles of one index of row name adapters whose slots lie on distinct indices of row. A tile's first tile_token_rows rows are prompt tokens, the rest padding.
All inputs are finite; a program needn't handle non-finite values.
Results may differ from the reference program's by a relative error of at most 0.02.
Values may be sent and summed in bfloat16 or wider, within the bound.
A program may use at most 64 MiB of HBM per device.

```python
import jax
import jax.numpy as jnp
from jax import lax

MODEL_WIDTH = 1600
HIDDEN_UNITS = 6400
QUERY_KEY_VALUE = 4800
ADAPTER_RANK = 16
ADP_DEV = 4
TILE = 128
TOK_ROW = 1024
ADAPTER_TOTAL = 32
TOKENS = 8192
TILES = 64


def route_tables(key):
    base_key = jax.random.fold_in(key, 7)
    key_slots, key_rows = jax.random.split(base_key, 2)
    slot_table = jax.random.permutation(key_slots, ADAPTER_TOTAL).astype(jnp.int32)
    owners = ADAPTER_TOTAL // ADP_DEV
    tiles_dev = TOK_ROW // TILE
    hot_slot = slot_table[ADAPTER_TOTAL - 1]
    hot_owner = hot_slot // ADP_DEV
    row_keys = jax.random.split(key_rows, TOKENS // TOK_ROW)

    def per_device(row_key):
        key_other, key_order, key_within = jax.random.split(row_key, 3)
        others = jax.random.permutation(key_other, owners - 1).astype(jnp.int32)
        others = others + (others >= hot_owner).astype(jnp.int32)
        chosen = jnp.concatenate([hot_owner[None].astype(jnp.int32), others[:tiles_dev - 1]])
        chosen = chosen[jax.random.permutation(key_order, tiles_dev)]
        within = jax.random.randint(key_within, (tiles_dev,), 0, ADP_DEV).astype(jnp.int32)
        within = jnp.where(chosen == hot_owner, hot_slot % ADP_DEV, within)
        return chosen * ADP_DEV + within
    slot_ids = jax.vmap(per_device)(row_keys).reshape(-1)
    inverse = jnp.argsort(slot_table, stable=True).astype(jnp.int32)
    return (slot_table, inverse[slot_ids].astype(jnp.int32))


def draw_adapter_storage_slot(key, part):
    return route_tables(key)[0]


def draw_tile_adapter_index(key, part):
    return route_tables(key)[1]


def draw_tile_token_rows(key, part):
    key_count, key_order = jax.random.split(jax.random.fold_in(key, 11), 2)
    counts = jax.random.randint(key_count, (TILES,), TILE // 2, TILE + 1).astype(jnp.int32)
    order_pick = jax.random.permutation(key_order, TILES)
    counts = counts.at[order_pick[0]].set(TILE).at[order_pick[1]].set(1)
    return counts.astype(jnp.int32)


def draw_hidden(key, part):
    key_base, key_col, key_row = jax.random.split(jax.random.fold_in(key, 13), 3)
    col_scale = jnp.exp(jax.random.uniform(key_col, (1, MODEL_WIDTH), minval=-1.15, maxval=1.15))
    row_scale = jnp.exp(jax.random.uniform(key_row, (TOKENS, 1), minval=-1.15, maxval=1.15))
    base_draw = jnp.clip(jax.random.normal(key_base, (TOKENS, MODEL_WIDTH)), -6.0, 6.0)
    return (base_draw * row_scale * col_scale).astype(jnp.float32).astype(jnp.bfloat16)


def levels(rng, dims, cuts, least, largest):
    def one(dim, blocks):
        heights = jax.random.uniform(jax.random.fold_in(jax.random.fold_in(rng, 6), dim), (blocks,), jnp.float32, least / len(cuts), largest / len(cuts))
        return jnp.repeat(jnp.exp(heights), dims[dim] // blocks).reshape((-1,) + (1,) * (len(dims) - dim - 1))

    loudness = one(*cuts[0])
    for cut in cuts[1:]:
        loudness = loudness * one(*cut)
    return loudness


def bell_draw(key, extent, spread, most, cuts=(), held_as=jnp.bfloat16):
    loudness = levels(key, extent, cuts, -0.22, 0.18) if cuts else 1.0
    values = jax.random.normal(key, extent, jnp.float32) * spread * loudness
    return jnp.minimum(jnp.maximum(values, -most), most).astype(held_as)


def setup_inputs(seed: int = 0) -> dict:
    streams_of = jax.random.split(jax.random.key(seed), 19)
    return {
        "hidden": draw_hidden(jax.random.fold_in(streams_of[18], 71), 0),
        "up_weight": bell_draw(streams_of[1], (MODEL_WIDTH, HIDDEN_UNITS), MODEL_WIDTH ** -0.5, 0.15625, ((0, 8), (1, 4))),
        "up_bias": bell_draw(streams_of[2], (HIDDEN_UNITS,), 0.5, 3.0, ((0, 4),), jnp.float32),
        "down_weight": bell_draw(streams_of[3], (HIDDEN_UNITS, MODEL_WIDTH), HIDDEN_UNITS ** -0.5, 0.078125, ((0, 4), (1, 8))),
        "down_bias": bell_draw(streams_of[4], (MODEL_WIDTH,), 0.5, 3.0, ((0, 4),), jnp.float32),
        "query_key_value_weight": bell_draw(streams_of[5], (MODEL_WIDTH, QUERY_KEY_VALUE), MODEL_WIDTH ** -0.5, 0.15625, ((0, 8), (1, 4))),
        "query_key_value_bias": bell_draw(streams_of[6], (QUERY_KEY_VALUE,), 0.5, 3.0, ((0, 4),), jnp.float32),
        "block_norm_gain": jnp.clip(1.0 + 0.18 * jax.random.normal(streams_of[7], (MODEL_WIDTH,), jnp.float32), 0.1, 1.9),
        "block_norm_shift": bell_draw(streams_of[8], (MODEL_WIDTH,), 0.5, 3.0, (), jnp.float32),
        "following_norm_gain": jnp.clip(1.0 + 0.18 * jax.random.normal(streams_of[9], (MODEL_WIDTH,), jnp.float32), 0.1, 1.9),
        "following_norm_shift": bell_draw(streams_of[10], (MODEL_WIDTH,), 0.5, 3.0, (), jnp.float32),
        "up_down_factors": bell_draw(streams_of[11], (ADAPTER_TOTAL, ADAPTER_RANK, MODEL_WIDTH), MODEL_WIDTH ** -0.5, 0.15625, ((0, 8),)),
        "up_up_factors": bell_draw(streams_of[12], (ADAPTER_TOTAL, ADAPTER_RANK, HIDDEN_UNITS), ADAPTER_RANK ** -0.5, 1.5, ((0, 8), (2, 4))),
        "query_key_value_down_factors": bell_draw(streams_of[13], (ADAPTER_TOTAL, ADAPTER_RANK, MODEL_WIDTH), MODEL_WIDTH ** -0.5, 0.15625, ((0, 8),)),
        "query_key_value_up_factors": bell_draw(streams_of[14], (ADAPTER_TOTAL, ADAPTER_RANK, QUERY_KEY_VALUE), ADAPTER_RANK ** -0.5, 1.5, ((0, 8), (2, 4))),
        "adapter_storage_slot": draw_adapter_storage_slot(jax.random.fold_in(streams_of[18], 71), 0),
        "tile_adapter_index": draw_tile_adapter_index(jax.random.fold_in(streams_of[18], 71), 0),
        "tile_token_rows": draw_tile_token_rows(jax.random.fold_in(streams_of[18], 71), 0),
    }


def layer_norm(values, gain_vec, shift_vec):
    row_mean = lax.optimization_barrier(jnp.mean(values, axis=-1, keepdims=True))
    centred = values - row_mean
    variance = lax.optimization_barrier(jnp.mean(centred * centred, axis=-1, keepdims=True))
    return centred * lax.rsqrt(variance + 1e-05) * gain_vec + shift_vec

def matrix_product_f32(left_op, right_op):
    return jnp.dot(left_op.astype(jnp.float32), right_op.astype(jnp.float32), preferred_element_type=jnp.float32)

def adapter_update(normalized_input, down_factor, up_factor, token_storage_slot):
    storage_slot_count, adapter_rank_size, embedding_width = down_factor.shape
    one_hot = (token_storage_slot[:, None] == jnp.arange(storage_slot_count, dtype=jnp.int32)[None, :]).astype(jnp.float32)
    every_low_rank = matrix_product_f32(normalized_input, down_factor.reshape(storage_slot_count * adapter_rank_size, embedding_width).T)
    every_low_rank = every_low_rank.reshape(-1, storage_slot_count, adapter_rank_size)
    low_rank = lax.optimization_barrier(jnp.sum(every_low_rank * one_hot[:, :, None], axis=1)).astype(jnp.bfloat16)
    broadcast_rows = (low_rank.astype(jnp.float32)[:, None, :] * one_hot[:, :, None]).reshape(-1, storage_slot_count * adapter_rank_size)
    update_rows = matrix_product_f32(broadcast_rows, up_factor.reshape(storage_slot_count * adapter_rank_size, -1)).astype(jnp.bfloat16)
    return lax.optimization_barrier(update_rows).astype(jnp.float32)

def reference(hidden, up_weight, up_bias, down_weight, down_bias, query_key_value_weight, query_key_value_bias, block_norm_gain, block_norm_shift, following_norm_gain, following_norm_shift, up_down_factors, up_up_factors, query_key_value_down_factors, query_key_value_up_factors, adapter_storage_slot, tile_adapter_index, tile_token_rows):
    tile_slot = adapter_storage_slot[tile_adapter_index].astype(jnp.int32)
    token_storage_slot = jnp.repeat(tile_slot, TILE)
    position = jnp.arange(TOKENS, dtype=jnp.int32) % TILE
    valid = (position < jnp.repeat(tile_token_rows, TILE))[:, None]
    normalized_input = layer_norm(hidden.astype(jnp.float32), block_norm_gain, block_norm_shift).astype(jnp.bfloat16)
    up_projection = matrix_product_f32(normalized_input, up_weight) + up_bias + adapter_update(normalized_input, up_down_factors, up_up_factors, token_storage_slot)
    activated = jax.nn.gelu(up_projection, approximate=True).astype(jnp.bfloat16)
    mixed = hidden.astype(jnp.float32) + matrix_product_f32(activated, down_weight) + down_bias
    h_out = jnp.where(valid, mixed, 0.0).astype(jnp.bfloat16)
    normalized_following = layer_norm(h_out.astype(jnp.float32), following_norm_gain, following_norm_shift).astype(jnp.bfloat16)
    projected_output = matrix_product_f32(normalized_following, query_key_value_weight) + query_key_value_bias + adapter_update(normalized_following, query_key_value_down_factors, query_key_value_up_factors, token_storage_slot)
    qkv = jnp.where(valid, projected_output, 0.0).astype(jnp.bfloat16)
    return (h_out, qkv)
```

```python
import functools
import jax
import jax.numpy as jnp
from jax import lax
from jax.experimental import pallas as pl
from jax.experimental.pallas import tpu as pltpu
from jax.sharding import PartitionSpec as P

MESH = pl.DeviceIdType.MESH


def gather_kernel(nw, nx, nz, *refs):
    ins, outs = refs[:nw], refs[nw:2 * nw]
    loc, zs, zr, xs, xr = refs[2 * nw:]
    row = lax.axis_index("row")
    z, x = row // nx, row % nx
    barrier = pltpu.get_barrier_semaphore()

    def peer(zz, xx):
        return {"row": zz * nx + xx}

    greet = [(z > 0, z - 1, x), (z < nz - 1, z + 1, x), (x > 0, z, x - 1), (x < nx - 1, z, x + 1)]
    total = jnp.int32(0)
    for ok, zz, xx in greet:
        total = total + ok.astype(jnp.int32)
        @pl.when(ok)
        def _():
            pl.semaphore_signal(barrier, inc=1, device_id=peer(zz, xx), device_id_type=MESH)
    pl.semaphore_wait(barrier, total)

    def copy(w, zz, xx, sem_s, sem_r, dz, dx, own=False):
        r = zz * nx + xx
        return pltpu.make_async_remote_copy(
            src_ref=ins[w] if own else outs[w].at[r], dst_ref=outs[w].at[r],
            send_sem=sem_s, recv_sem=sem_r, device_id=peer(dz, dx), device_id_type=MESH)

    pend = []

    def send(ok, cp):
        @pl.when(ok)
        def _():
            cp.start()
        pend.append((ok, cp))

    def recv(ok, cp):
        @pl.when(ok)
        def _():
            cp.wait_recv()

    def xsend(w, s, d, zz, ok, own):
        k = 2 * s + d
        send(ok & (x < nx - 1), copy(w, zz, x, xs.at[w, 0, 0, k], xr.at[w, 0, 0, k], z, x + 1, own))
        send(ok & (x > 0), copy(w, zz, x, xs.at[w, 0, 1, k], xr.at[w, 0, 1, k], z, x - 1, own))

    true = z >= 0
    locs = []
    for w in range(nw):
        c = pltpu.make_async_copy(ins[w], outs[w].at[row], loc.at[w])
        c.start()
        locs.append(c)
    for w in range(nw):
        for s in range(nz):
            if s > 0:
                recv(z - s >= 0, copy(w, z - s, x, zs.at[w, 0, s], zr.at[w, 0, s], z, x))
                recv(z + s < nz, copy(w, z + s, x, zs.at[w, 1, s], zr.at[w, 1, s], z, x))
            if s < nz - 1:
                send((z - s >= 0) & (z < nz - 1), copy(w, z - s, x, zs.at[w, 0, s + 1], zr.at[w, 0, s + 1], z + 1, x, s == 0))
                send((z + s < nz) & (z > 0), copy(w, z + s, x, zs.at[w, 1, s + 1], zr.at[w, 1, s + 1], z - 1, x, s == 0))
            for d in range(2 if s else 1):
                zz = z - s if d == 0 else z + s
                xsend(w, s, d, zz, (zz >= 0) & (zz < nz), s == 0)
            if s == 0 and w == 0:
                pass
    for w in range(nw):
        for t in range(1, nx):
            for s in range(nz):
                for d in range(2 if s else 1):
                    zz = z - s if d == 0 else z + s
                    ok = (zz >= 0) & (zz < nz)
                    k = 2 * s + d
                    for side in range(2):
                        xx = x - t if side == 0 else x + t
                        okx = ok & ((xx >= 0) & (xx < nx))
                        recv(okx, copy(w, zz, xx, xs.at[w, t - 1, side, k], xr.at[w, t - 1, side, k], z, x))
                        if t < nx - 1:
                            nxt = x + 1 if side == 0 else x - 1
                            send(okx & (nxt >= 0) & (nxt < nx),
                                 copy(w, zz, xx, xs.at[w, t, side, k], xr.at[w, t, side, k], z, nxt))
    for c in locs:
        c.wait()
    for ok, cp in pend:
        @pl.when(ok)
        def _():
            cp.wait_send()


def gather_weights(ws, nx, nz, cid=3):
    nw = len(ws)
    n = nx * nz
    D = pltpu.SemaphoreType.DMA
    return pl.pallas_call(
        functools.partial(gather_kernel, nw, nx, nz),
        out_shape=[jax.ShapeDtypeStruct((n,) + w.shape, w.dtype) for w in ws],
        in_specs=[pl.BlockSpec(memory_space=pl.ANY)] * nw,
        out_specs=[pl.BlockSpec(memory_space=pl.ANY)] * nw,
        scratch_shapes=[D((nw,)), D((nw, 2, nz)), D((nw, 2, nz)),
                        D((nw, nx - 1, 2, 2 * nz)), D((nw, nx - 1, 2, 2 * nz))],
        compiler_params=pltpu.CompilerParams(collective_id=cid, has_side_effects=True),
    )(*ws)


def layer_norm(values, gain_vec, shift_vec):
    row_mean = jnp.mean(values, axis=-1, keepdims=True)
    centred = values - row_mean
    variance = jnp.mean(centred * centred, axis=-1, keepdims=True)
    return centred * lax.rsqrt(variance + 1e-05) * gain_vec + shift_vec


def adapter_update(normalized, down_tile, up_tile):
    tiles = down_tile.shape[0]
    tiled = normalized.reshape(tiles, -1, normalized.shape[1])
    low = jnp.einsum("tid,tcd->tic", tiled, down_tile, preferred_element_type=jnp.float32)
    delta = jnp.einsum(
        "tic,tcf->tif", low.astype(jnp.bfloat16), up_tile, preferred_element_type=jnp.float32
    )
    return delta.astype(jnp.bfloat16).reshape(normalized.shape[0], -1).astype(jnp.float32)


def fetch_adapters(factors, adapter_storage_slot, tile_adapter_index):
    per_holder = factors[0].shape[0]
    rows = lax.axis_size("row")
    me = lax.axis_index("row")
    adapters = jnp.arange(adapter_storage_slot.shape[0], dtype=jnp.int32)

    def slots_of(indices):
        pick = (indices[..., None] == adapters).astype(jnp.int32)
        return jnp.sum(pick * adapter_storage_slot, axis=-1)

    every = slots_of(lax.all_gather(tile_adapter_index, "row", axis=0, tiled=False))
    mine = slots_of(tile_adapter_index)
    residents = me * per_holder + jnp.arange(per_holder, dtype=jnp.int32)
    wanted = jnp.any(every[:, :, None] == residents, axis=1).astype(jnp.bfloat16)
    stacked = jnp.concatenate(factors, axis=2)
    outgoing = jnp.einsum(
        "rf,fcd->rcd", wanted, stacked, preferred_element_type=jnp.float32
    ).astype(jnp.bfloat16)
    arrived = lax.all_to_all(outgoing, "row", split_axis=0, concat_axis=0, tiled=True)
    holder = (mine[:, None] // per_holder == jnp.arange(rows, dtype=jnp.int32)).astype(jnp.bfloat16)
    chosen = jnp.einsum(
        "to,ocd->tcd", holder, arrived, preferred_element_type=jnp.float32
    ).astype(jnp.bfloat16)
    widths = [f.shape[2] for f in factors]
    ends = [sum(widths[: i + 1]) for i in range(len(widths))]
    return [chosen[:, :, e - w : e] for w, e in zip(widths, ends)]


def per_device(
    nx,
    nz,
    hidden,
    up_weight,
    up_bias,
    down_weight,
    down_bias,
    query_key_value_weight,
    query_key_value_bias,
    block_norm_gain,
    block_norm_shift,
    following_norm_gain,
    following_norm_shift,
    up_down_factors,
    up_up_factors,
    query_key_value_down_factors,
    query_key_value_up_factors,
    adapter_storage_slot,
    tile_adapter_index,
    tile_token_rows,
):
    tok_rows = hidden.shape[0]
    tile_len = tok_rows // tile_adapter_index.shape[0]
    valid = (jnp.arange(tile_len, dtype=jnp.int32)[None, :] < tile_token_rows[:, None]).reshape(
        tok_rows, 1
    )
    up_down, up_up, qkv_down, qkv_up = fetch_adapters(
        [up_down_factors, up_up_factors, query_key_value_down_factors, query_key_value_up_factors],
        adapter_storage_slot,
        tile_adapter_index,
    )
    up_all, down_all, qkv_all = gather_weights(
        [up_weight, down_weight.T, query_key_value_weight], nx, nz
    )
    up_all, down_all, qkv_all = [w.reshape(-1, w.shape[2]) for w in (up_all, down_all, qkv_all)]
    gathered = lax.all_gather(hidden, "col", axis=1, tiled=True)
    normalized = layer_norm(
        gathered.astype(jnp.float32), block_norm_gain, block_norm_shift
    ).astype(jnp.bfloat16)
    up_projection = (
        jnp.dot(normalized, up_all, preferred_element_type=jnp.float32)
        + up_bias
        + adapter_update(normalized, up_down, up_up)
    )
    activated = jax.nn.gelu(up_projection, approximate=True).astype(jnp.bfloat16)
    partial_value = lax.dot_general(
        activated, down_all, (((1,), (1,)), ((), ())), preferred_element_type=jnp.float32
    )
    summed = lax.psum_scatter(
        partial_value.astype(jnp.bfloat16), "col", scatter_dimension=1, tiled=True
    ).astype(jnp.float32)
    mixed = hidden.astype(jnp.float32) + summed + down_bias
    h_out = jnp.where(valid, mixed, 0.0).astype(jnp.bfloat16)
    gathered_next = lax.all_gather(h_out, "col", axis=1, tiled=True)
    normalized_next = layer_norm(
        gathered_next.astype(jnp.float32), following_norm_gain, following_norm_shift
    ).astype(jnp.bfloat16)
    projected = (
        jnp.dot(normalized_next, qkv_all, preferred_element_type=jnp.float32)
        + query_key_value_bias
        + adapter_update(normalized_next, qkv_down, qkv_up)
    )
    qkv = jnp.where(valid, projected, 0.0).astype(jnp.bfloat16)
    return (h_out, qkv)


def solution(mesh):
    nx = max(mesh.shape["col"] // 2, 1)
    nz = mesh.shape["row"] // nx
    in_specs = (
        P("row", "col"),
        P("row", "col"),
        P("col"),
        P("col", "row"),
        P("col"),
        P("row", "col"),
        P("col"),
        P(),
        P(),
        P(),
        P(),
        P("row", None, None),
        P("row", None, "col"),
        P("row", None, None),
        P("row", None, "col"),
        P(),
        P("row"),
        P("row"),
    )
    return jax.shard_map(
        functools.partial(per_device, nx, nz),
        mesh=mesh,
        in_specs=in_specs,
        out_specs=(P("row", "col"), P("row", "col")),
        check_vma=False,
    )
```

```python
import functools
import jax
import jax.numpy as jnp
from jax import lax
from jax.experimental import pallas as pl
from jax.experimental.pallas import tpu as pltpu
from jax.sharding import PartitionSpec as P

MESH = pl.DeviceIdType.MESH


def fused_kernel(
    nx, nz, nc, tile, chunk,
    holder, hid_in, up_in, dn_in, qk_in, fd_in, fu_in, fq_in, up_bias, dn_bias, qk_bias,
    gain1, shift1, gain2, shift2, valid,
    h_out, qkv_out,
    upw, dnw, qkw, hid, norm, act, part, rsb, nxt, fd, fu, fq, acc, feat,
    loc, zs, zr, xs, xr, hs, hr, ads, adr, rss, rsr, ags, agr,
):
    nr = nx * nz
    per = nr // nc
    rows, width = hid_in.shape
    piece = up_in.shape[0]
    model = width * nc
    chunks = rows // chunk
    row, col = lax.axis_index("row"), lax.axis_index("col")
    z, x = row // nx, row % nx
    barrier = pltpu.get_barrier_semaphore()

    @pl.loop(1, nr)
    def _(k):
        pl.semaphore_signal(barrier, inc=1, device_id={"row": lax.rem(row + k, nr)}, device_id_type=MESH)

    @pl.loop(1, nc)
    def _(k):
        pl.semaphore_signal(barrier, inc=1, device_id={"col": lax.rem(col + k, nc)}, device_id_type=MESH)

    pl.semaphore_wait(barrier, nr + nc - 2)
    ins, outs = (up_in, dn_in, qk_in), (upw, dnw, qkw)

    def copy(w, zz, xx, sem_s, sem_r, dz, dx, own=False):
        r = zz * nx + xx
        return pltpu.make_async_remote_copy(
            src_ref=ins[w] if own else outs[w].at[r], dst_ref=outs[w].at[r],
            send_sem=sem_s, recv_sem=sem_r,
            device_id={"row": dz * nx + dx}, device_id_type=MESH)

    pend = []

    def send(ok, cp):
        @pl.when(ok)
        def _():
            cp.start()
        pend.append((ok, cp))

    def recv(ok, cp):
        @pl.when(ok)
        def _():
            cp.wait_recv()

    def zstep(w, s):
        if s > 0:
            recv(z - s >= 0, copy(w, z - s, x, zs.at[w, 0, s], zr.at[w, 0, s], z, x))
            recv(z + s < nz, copy(w, z + s, x, zs.at[w, 1, s], zr.at[w, 1, s], z, x))
        if s < nz - 1:
            send((z - s >= 0) & (z < nz - 1), copy(w, z - s, x, zs.at[w, 0, s + 1], zr.at[w, 0, s + 1], z + 1, x, s == 0))
            send((z + s < nz) & (z > 0), copy(w, z + s, x, zs.at[w, 1, s + 1], zr.at[w, 1, s + 1], z - 1, x, s == 0))
        for d in range(2 if s else 1):
            zz = z - s if d == 0 else z + s
            ok = (zz >= 0) & (zz < nz)
            k = 2 * s + d
            send(ok & (x < nx - 1), copy(w, zz, x, xs.at[w, 0, 0, k], xr.at[w, 0, 0, k], z, x + 1, s == 0))
            send(ok & (x > 0), copy(w, zz, x, xs.at[w, 0, 1, k], xr.at[w, 0, 1, k], z, x - 1, s == 0))

    def xfinish(w):
        for t in range(1, nx):
            for s in range(nz):
                for d in range(2 if s else 1):
                    zz = z - s if d == 0 else z + s
                    ok = (zz >= 0) & (zz < nz)
                    k = 2 * s + d
                    for side in range(2):
                        xx = x - t if side == 0 else x + t
                        okx = ok & (xx >= 0) & (xx < nx)
                        recv(okx, copy(w, zz, xx, xs.at[w, t - 1, side, k], xr.at[w, t - 1, side, k], z, x))
                        if t < nx - 1:
                            to = x + 1 if side == 0 else x - 1
                            send(okx & (to >= 0) & (to < nx),
                                 copy(w, zz, xx, xs.at[w, t, side, k], xr.at[w, t, side, k], z, to))

    def col_copy(src, dst, ss, rs, k):
        return pltpu.make_async_remote_copy(
            src_ref=src, dst_ref=dst, send_sem=ss, recv_sem=rs,
            device_id={"col": lax.rem(col + k, nc)}, device_id_type=MESH)

    def hid_copy(k):
        return col_copy(hid_in, hid.at[col], hs.at[k], hr.at[k], k)

    def adapter_copy(i, k):
        src, dst = ((fd_in, fd), (fu_in, fu), (fq_in, fq))[i]
        to = lax.rem(row + k, nr)
        return pltpu.make_async_remote_copy(
            src_ref=src.at[to], dst_ref=dst.at[row], send_sem=ads.at[i, k], recv_sem=adr.at[i, k],
            device_id={"row": to}, device_id_type=MESH)

    def span(i):
        return pl.ds(pl.multiple_of(i * chunk, chunk), chunk)

    def rs_copy(i, k):
        to = lax.rem(col + k, nc)
        return col_copy(part.at[to, span(i)], rsb.at[col, span(i)], rss.at[i, k], rsr.at[i, k], k)

    def ag_copy(i, k):
        return col_copy(nxt.at[col, span(i)], nxt.at[col, span(i)], ags.at[i, k], agr.at[i, k], k)

    locs = [pltpu.make_async_copy(s, d.at[row], loc.at[i]) for i, (s, d) in enumerate(zip(ins, outs))]
    locs.append(pltpu.make_async_copy(hid_in, hid.at[col], loc.at[3]))
    for i, (s, d) in enumerate(((fd_in, fd), (fu_in, fu), (fq_in, fq))):
        locs.append(pltpu.make_async_copy(s.at[row], d.at[row], loc.at[4 + i]))
    zstep(0, 0)
    for k in range(1, nc):
        hid_copy(k).start()

    @pl.loop(1, nr)
    def _(k):
        for i in range(3):
            adapter_copy(i, k).start()

    for c in locs:
        c.start()

    def normalize(i, source, gain, shift):
        vals = [source[c, span(i), :].astype(jnp.float32) for c in range(nc)]
        mean = sum(jnp.sum(v, axis=1, keepdims=True) for v in vals) / model
        vals = [v - mean for v in vals]
        var = sum(jnp.sum(v * v, axis=1, keepdims=True) for v in vals) / model
        scale = lax.rsqrt(var + 1e-05)
        for c in range(nc):
            feat[...] = vals[c] * scale * gain[c] + shift[c]
            for j in range(per):
                norm[per * c + j, span(i), :] = feat[:, j * piece:(j + 1) * piece].astype(jnp.bfloat16)

    def project(i, weights, kind, ups, bias, out_width):
        total = jnp.zeros((chunk, out_width), jnp.float32)
        for r in range(nr):
            total = total + jnp.dot(norm[r, span(i), :], weights[r], preferred_element_type=jnp.float32)
        acc[:, :out_width] = total + bias[...]
        for j in range(chunk // tile):
            owner = holder[i * (chunk // tile) + j]
            downs = fd[owner, kind]
            up = ups[owner]
            here = pl.ds(pl.multiple_of(i * chunk + j * tile, tile), tile)
            low = jnp.zeros((tile, downs.shape[1]), jnp.float32)
            for r in range(nr):
                low = low + lax.dot_general(
                    norm[r, here, :], downs[r], (((1,), (1,)), ((), ())),
                    preferred_element_type=jnp.float32)
            delta = jnp.dot(low.astype(jnp.bfloat16), up, preferred_element_type=jnp.float32)
            acc[j * tile:(j + 1) * tile, :out_width] += delta.astype(jnp.bfloat16).astype(jnp.float32)

    def up_stage(i):
        project(i, upw, 0, fu, up_bias, act.shape[1])
        act[span(i), :] = jax.nn.gelu(acc[:, :act.shape[1]], approximate=True).astype(jnp.bfloat16)

    def down_stage(i):
        for c in range(nc):
            for j in range(per):
                feat[:, j * piece:(j + 1) * piece] = lax.dot_general(
                    act[span(i), :], dnw[per * c + j], (((1,), (1,)), ((), ())),
                    preferred_element_type=jnp.float32)
            part[c, span(i), :] = feat[...].astype(jnp.bfloat16)
        for k in range(1, nc):
            rs_copy(i, k).start()

    def mix_stage(i):
        for k in range(1, nc):
            rs_copy(i, k).wait_recv()
        total = part[col, span(i), :].astype(jnp.float32)
        for k in range(1, nc):
            total = total + rsb[lax.rem(col + k, nc), span(i), :].astype(jnp.float32)
        mixed = hid[col, span(i), :].astype(jnp.float32) + total + dn_bias[...]
        new = jnp.where(valid[span(i), :] > 0, mixed, 0.0).astype(jnp.bfloat16)
        h_out[span(i), :] = new
        nxt[col, span(i), :] = new
        for k in range(1, nc):
            ag_copy(i, k).start()

    def qkv_stage(i):
        for k in range(1, nc):
            ag_copy(i, k).wait_recv()
        normalize(i, nxt, gain2, shift2)
        wide = qkv_out.shape[1]
        project(i, qkw, 1, fq, qk_bias, wide)
        qkv_out[span(i), :] = jnp.where(valid[span(i), :] > 0, acc[:, :wide], 0.0).astype(jnp.bfloat16)

    def every(first, last, stage):
        lax.fori_loop(first, last, lambda i, c: (stage(i), c)[1], 0)

    for s in range(1, nz - 1):
        zstep(0, s)
    locs[3].wait()
    for k in range(1, nc):
        hid_copy(k).wait_recv()
    every(0, chunks, lambda i: normalize(i, hid, gain1, shift1))
    zstep(0, nz - 1)
    zstep(1, 0)

    @pl.loop(1, nr)
    def _(k):
        for i in range(3):
            adapter_copy(i, k).wait_recv()

    for c in locs[:3] + locs[4:]:
        c.wait()
    zstep(1, 1)
    xfinish(0)
    every(0, chunks // 2, up_stage)
    for s in range(2, nz):
        zstep(1, s)
    zstep(2, 0)
    every(chunks // 2, chunks, up_stage)
    for s in range(1, nz):
        zstep(2, s)
    xfinish(1)
    every(0, chunks, down_stage)
    every(0, chunks, mix_stage)
    xfinish(2)
    every(0, chunks, qkv_stage)

    for ok, cp in pend:
        @pl.when(ok)
        def _():
            cp.wait_send()
    for k in range(1, nc):
        hid_copy(k).wait_send()

    @pl.loop(1, nr)
    def _(k):
        for i in range(3):
            adapter_copy(i, k).wait_send()

    @pl.loop(0, chunks)
    def _(i):
        for k in range(1, nc):
            rs_copy(i, k).wait_send()
            ag_copy(i, k).wait_send()


def fetch_adapters(factors, adapter_storage_slot, tile_adapter_index):
    per_holder = factors[0].shape[0]
    rows = lax.axis_size("row")
    me = lax.axis_index("row")
    adapters = jnp.arange(adapter_storage_slot.shape[0], dtype=jnp.int32)

    def slots_of(indices):
        pick = (indices[..., None] == adapters).astype(jnp.int32)
        return jnp.sum(pick * adapter_storage_slot, axis=-1)

    every = slots_of(lax.all_gather(tile_adapter_index, "row", axis=0, tiled=False))
    mine = slots_of(tile_adapter_index)
    residents = me * per_holder + jnp.arange(per_holder, dtype=jnp.int32)
    wanted = jnp.any(every[:, :, None] == residents, axis=1).astype(jnp.bfloat16)
    picked = [
        jnp.einsum("rf,fcd->rcd", wanted, f, preferred_element_type=jnp.float32).astype(jnp.bfloat16)
        for f in factors
    ]
    return picked, mine // per_holder


def per_device(
    nx,
    nz,
    hidden,
    up_weight,
    up_bias,
    down_weight,
    down_bias,
    query_key_value_weight,
    query_key_value_bias,
    block_norm_gain,
    block_norm_shift,
    following_norm_gain,
    following_norm_shift,
    up_down_factors,
    up_up_factors,
    query_key_value_down_factors,
    query_key_value_up_factors,
    adapter_storage_slot,
    tile_adapter_index,
    tile_token_rows,
):
    tok_rows, width = hidden.shape
    tile_len = tok_rows // tile_adapter_index.shape[0]
    nr, nc = nx * nz, lax.axis_size("col")
    piece = up_weight.shape[0]
    valid = (jnp.arange(tile_len, dtype=jnp.int32)[None, :] < tile_token_rows[:, None]).reshape(
        tok_rows, 1
    )
    (up_down, up_up, qkv_down, qkv_up), holder = fetch_adapters(
        [up_down_factors, up_up_factors, query_key_value_down_factors, query_key_value_up_factors],
        adapter_storage_slot,
        tile_adapter_index,
    )
    rank = up_down.shape[1]
    downs = jnp.stack([up_down, qkv_down], axis=1).reshape(nr, 2, rank, nr, piece)
    downs = downs.transpose(0, 1, 3, 2, 4)
    chunk = min(2 * tile_len, tok_rows)
    chunks = tok_rows // chunk
    hu, qc = up_weight.shape[1], query_key_value_weight.shape[1]
    dma = pltpu.SemaphoreType.DMA
    bf, f32 = jnp.bfloat16, jnp.float32
    anywhere = pl.BlockSpec(memory_space=pl.ANY)
    vmem = pl.BlockSpec(memory_space=pltpu.VMEM)
    return tuple(pl.pallas_call(
        functools.partial(fused_kernel, nx, nz, nc, tile_len, chunk),
        out_shape=[
            jax.ShapeDtypeStruct((tok_rows, width), bf),
            jax.ShapeDtypeStruct((tok_rows, qc), bf),
        ],
        in_specs=[pl.BlockSpec(memory_space=pltpu.SMEM)] + [anywhere] * 7 + [vmem] * 8,
        out_specs=[vmem, vmem],
        scratch_shapes=[
            pltpu.VMEM((nr, piece, hu), bf),
            pltpu.VMEM((nr, piece, hu), bf),
            pltpu.VMEM((nr, piece, qc), bf),
            pltpu.VMEM((nc, tok_rows, width), bf),
            pltpu.VMEM((nr, tok_rows, piece), bf),
            pltpu.VMEM((tok_rows, hu), bf),
            pltpu.VMEM((nc, tok_rows, width), bf),
            pltpu.VMEM((nc, tok_rows, width), bf),
            pltpu.VMEM((nc, tok_rows, width), bf),
            pltpu.VMEM(downs.shape, bf),
            pltpu.VMEM(up_up.shape, bf),
            pltpu.VMEM(qkv_up.shape, bf),
            pltpu.VMEM((chunk, max(hu, qc)), f32),
            pltpu.VMEM((chunk, width), f32),
            dma((7,)),
            dma((3, 2, nz)), dma((3, 2, nz)),
            dma((3, nx - 1, 2, 2 * nz)), dma((3, nx - 1, 2, 2 * nz)),
            dma((nc,)), dma((nc,)),
            dma((3, nr)), dma((3, nr)),
            dma((chunks, nc)), dma((chunks, nc)),
            dma((chunks, nc)), dma((chunks, nc)),
        ],
        compiler_params=pltpu.CompilerParams(
            collective_id=5, has_side_effects=True, vmem_limit_bytes=62 * 1024 * 1024
        ),
    )(
        holder, hidden, up_weight, down_weight.T, query_key_value_weight, downs, up_up, qkv_up,
        up_bias[None], down_bias[None], query_key_value_bias[None],
        block_norm_gain.reshape(nc, 1, width), block_norm_shift.reshape(nc, 1, width),
        following_norm_gain.reshape(nc, 1, width), following_norm_shift.reshape(nc, 1, width),
        valid.astype(jnp.int32),
    ))


def solution(mesh):
    nx = max(mesh.shape["col"] // 2, 1)
    nz = mesh.shape["row"] // nx
    in_specs = (
        P("row", "col"),
        P("row", "col"),
        P("col"),
        P("col", "row"),
        P("col"),
        P("row", "col"),
        P("col"),
        P(),
        P(),
        P(),
        P(),
        P("row", None, None),
        P("row", None, "col"),
        P("row", None, None),
        P("row", None, "col"),
        P(),
        P("row"),
        P("row"),
    )
    return jax.shard_map(
        functools.partial(per_device, nx, nz),
        mesh=mesh,
        in_specs=in_specs,
        out_specs=(P("row", "col"), P("row", "col")),
        check_vma=False,
    )
```

```python
import functools
import jax
import jax.numpy as jnp
from jax import lax
from jax.experimental import pallas as pl
from jax.experimental.pallas import tpu as pltpu
from jax.sharding import PartitionSpec as P

MESH = pl.DeviceIdType.MESH


def fused_kernel(
    nx, nz, nc, tile, chunk,
    holder, hid_in, up_in, dn_in, qk_in, fd_in, fu_in, fq_in, up_bias, dn_bias, qk_bias,
    norms, valid,
    h_out, qkv_out,
    upw, dnw, qkw, hid, norm, act, part, rsb, nxt, fd, fu, fq, acc, feat,
    loc, zs, zr, xs, xr, hs, hr, ads, adr, rss, rsr, ags, agr,
):
    nr = nx * nz
    per = nr // nc
    rows, width = hid_in.shape
    piece = up_in.shape[0]
    model = width * nc
    chunks = rows // chunk
    row, col = lax.axis_index("row"), lax.axis_index("col")
    z, x = row // nx, row % nx
    barrier = pltpu.get_barrier_semaphore()

    @pl.loop(1, nr)
    def _(k):
        pl.semaphore_signal(barrier, inc=1, device_id={"row": lax.rem(row + k, nr)}, device_id_type=MESH)

    @pl.loop(1, nc)
    def _(k):
        pl.semaphore_signal(barrier, inc=1, device_id={"col": lax.rem(col + k, nc)}, device_id_type=MESH)

    pl.semaphore_wait(barrier, nr + nc - 2)
    ins, outs = (up_in, dn_in, qk_in), (upw, dnw, qkw)

    def copy(w, zz, xx, sem_s, sem_r, dz, dx, own=False):
        r = zz * nx + xx
        return pltpu.make_async_remote_copy(
            src_ref=ins[w] if own else outs[w].at[r], dst_ref=outs[w].at[r],
            send_sem=sem_s, recv_sem=sem_r,
            device_id={"row": dz * nx + dx}, device_id_type=MESH)

    pend = []

    def send(ok, cp):
        @pl.when(ok)
        def _():
            cp.start()
        pend.append((ok, cp))

    def recv(ok, cp):
        @pl.when(ok)
        def _():
            cp.wait_recv()

    def zpart(w, s):
        if s > 0:
            recv(z - s >= 0, copy(w, z - s, x, zs.at[w, 0, s], zr.at[w, 0, s], z, x))
            recv(z + s < nz, copy(w, z + s, x, zs.at[w, 1, s], zr.at[w, 1, s], z, x))
        if s < nz - 1:
            send((z - s >= 0) & (z < nz - 1), copy(w, z - s, x, zs.at[w, 0, s + 1], zr.at[w, 0, s + 1], z + 1, x, s == 0))
            send((z + s < nz) & (z > 0), copy(w, z + s, x, zs.at[w, 1, s + 1], zr.at[w, 1, s + 1], z - 1, x, s == 0))

    def xpart(w, s):
        for d in range(2 if s else 1):
            zz = z - s if d == 0 else z + s
            ok = (zz >= 0) & (zz < nz)
            k = 2 * s + d
            send(ok & (x < nx - 1), copy(w, zz, x, xs.at[w, 0, 0, k], xr.at[w, 0, 0, k], z, x + 1, s == 0))
            send(ok & (x > 0), copy(w, zz, x, xs.at[w, 0, 1, k], xr.at[w, 0, 1, k], z, x - 1, s == 0))

    def zstep(w, s):
        zpart(w, s)
        xpart(w, s)

    def xfinish(w):
        for t in range(1, nx):
            for s in range(nz):
                for d in range(2 if s else 1):
                    zz = z - s if d == 0 else z + s
                    ok = (zz >= 0) & (zz < nz)
                    k = 2 * s + d
                    for side in range(2):
                        xx = x - t if side == 0 else x + t
                        okx = ok & (xx >= 0) & (xx < nx)
                        recv(okx, copy(w, zz, xx, xs.at[w, t - 1, side, k], xr.at[w, t - 1, side, k], z, x))
                        if t < nx - 1:
                            to = x + 1 if side == 0 else x - 1
                            send(okx & (to >= 0) & (to < nx),
                                 copy(w, zz, xx, xs.at[w, t, side, k], xr.at[w, t, side, k], z, to))

    def col_copy(src, dst, ss, rs, k):
        return pltpu.make_async_remote_copy(
            src_ref=src, dst_ref=dst, send_sem=ss, recv_sem=rs,
            device_id={"col": lax.rem(col + k, nc)}, device_id_type=MESH)

    def hid_copy(k):
        return col_copy(hid_in, hid.at[col], hs.at[k], hr.at[k], k)

    def adapter_copy(i, k):
        src, dst = ((fd_in, fd), (fu_in, fu), (fq_in, fq))[i]
        to = lax.rem(row + k, nr)
        return pltpu.make_async_remote_copy(
            src_ref=src.at[to], dst_ref=dst.at[row], send_sem=ads.at[i, k], recv_sem=adr.at[i, k],
            device_id={"row": to}, device_id_type=MESH)

    def span(i):
        return pl.ds(pl.multiple_of(i * chunk, chunk), chunk)

    def rs_copy(i, k):
        to = lax.rem(col + k, nc)
        return col_copy(part.at[to, span(i)], rsb.at[col, span(i)], rss.at[i, k], rsr.at[i, k], k)

    def ag_copy(i, k):
        return col_copy(nxt.at[col, span(i)], nxt.at[col, span(i)], ags.at[i, k], agr.at[i, k], k)

    locs = [pltpu.make_async_copy(s, d.at[row], loc.at[i]) for i, (s, d) in enumerate(zip(ins, outs))]
    locs.append(pltpu.make_async_copy(hid_in, hid.at[col], loc.at[3]))
    for i, (s, d) in enumerate(((fd_in, fd), (fu_in, fu), (fq_in, fq))):
        locs.append(pltpu.make_async_copy(s.at[row], d.at[row], loc.at[4 + i]))
    zstep(0, 0)
    for k in range(1, nc):
        hid_copy(k).start()

    @pl.loop(1, nr)
    def _(k):
        for i in range(3):
            adapter_copy(i, k).start()

    for c in locs:
        c.start()

    def normalize(i, source, base):
        vals = [source[c, span(i), :].astype(jnp.float32) for c in range(nc)]
        mean = sum(jnp.sum(v, axis=1, keepdims=True) for v in vals) / model
        vals = [v - mean for v in vals]
        var = sum(jnp.sum(v * v, axis=1, keepdims=True) for v in vals) / model
        scale = lax.rsqrt(var + 1e-05)
        for c in range(nc):
            feat[...] = vals[c] * scale * norms[base + c] + norms[base + nc + c]
            for j in range(per):
                norm[per * c + j, span(i), :] = feat[:, j * piece:(j + 1) * piece].astype(jnp.bfloat16)

    def project(i, weights, kind, ups, bias, out_width):
        total = jnp.zeros((chunk, out_width), jnp.float32)
        for r in range(nr):
            total = total + jnp.dot(norm[r, span(i), :], weights[r], preferred_element_type=jnp.float32)
        acc[:, :out_width] = total + bias[...]
        for j in range(chunk // tile):
            owner = holder[i * (chunk // tile) + j]
            downs = fd[owner, kind]
            up = ups[owner]
            here = pl.ds(pl.multiple_of(i * chunk + j * tile, tile), tile)
            low = jnp.zeros((tile, downs.shape[1]), jnp.float32)
            for r in range(nr):
                low = low + lax.dot_general(
                    norm[r, here, :], downs[r], (((1,), (1,)), ((), ())),
                    preferred_element_type=jnp.float32)
            delta = jnp.dot(low.astype(jnp.bfloat16), up, preferred_element_type=jnp.float32)
            acc[j * tile:(j + 1) * tile, :out_width] += delta.astype(jnp.bfloat16).astype(jnp.float32)

    def up_stage(i):
        project(i, upw, 0, fu, up_bias, act.shape[1])
        act[span(i), :] = jax.nn.gelu(acc[:, :act.shape[1]], approximate=True).astype(jnp.bfloat16)

    def down_stage(i):
        for c in range(nc):
            for j in range(per):
                feat[:, j * piece:(j + 1) * piece] = lax.dot_general(
                    act[span(i), :], dnw[per * c + j], (((1,), (1,)), ((), ())),
                    preferred_element_type=jnp.float32)
            part[c, span(i), :] = feat[...].astype(jnp.bfloat16)
        for k in range(1, nc):
            rs_copy(i, k).start()

    def mix_stage(i):
        for k in range(1, nc):
            rs_copy(i, k).wait_recv()
        total = part[col, span(i), :].astype(jnp.float32)
        for k in range(1, nc):
            total = total + rsb[lax.rem(col + k, nc), span(i), :].astype(jnp.float32)
        mixed = hid[col, span(i), :].astype(jnp.float32) + total + dn_bias[...]
        new = jnp.where(valid[span(i), :] > 0, mixed, 0.0).astype(jnp.bfloat16)
        h_out[span(i), :] = new
        nxt[col, span(i), :] = new
        for k in range(1, nc):
            ag_copy(i, k).start()

    def qkv_stage(i):
        for k in range(1, nc):
            ag_copy(i, k).wait_recv()
        normalize(i, nxt, 2 * nc)
        wide = qkv_out.shape[1]
        project(i, qkw, 1, fq, qk_bias, wide)
        qkv_out[span(i), :] = jnp.where(valid[span(i), :] > 0, acc[:, :wide], 0.0).astype(jnp.bfloat16)

    def every(first, last, stage):
        lax.fori_loop(first, last, lambda i, c: (stage(i), c)[1], 0)

    for s in range(1, nz):
        zstep(0, s)
        if s == 1:
            zpart(1, 0)
    xpart(1, 0)
    zpart(1, 1)
    zpart(2, 0)
    locs[3].wait()
    for k in range(1, nc):
        hid_copy(k).wait_recv()
    every(0, chunks, lambda i: normalize(i, hid, 0))

    @pl.loop(1, nr)
    def _(k):
        for i in range(3):
            adapter_copy(i, k).wait_recv()

    for c in locs[:3] + locs[4:]:
        c.wait()
    xfinish(0)
    xpart(1, 1)
    every(0, chunks // 2, up_stage)
    for s in range(2, nz):
        zstep(1, s)
    every(chunks // 2, chunks, up_stage)
    for s in range(1, nz - 1):
        zpart(2, s)
    xpart(2, 0)
    xfinish(1)
    for s in range(1, nz - 1):
        xpart(2, s)
    every(0, chunks // 2, down_stage)
    zstep(2, nz - 1)
    every(chunks // 2, chunks, down_stage)
    every(0, chunks, mix_stage)
    xfinish(2)
    every(0, chunks, qkv_stage)

    for ok, cp in pend:
        @pl.when(ok)
        def _():
            cp.wait_send()
    for k in range(1, nc):
        hid_copy(k).wait_send()

    @pl.loop(1, nr)
    def _(k):
        for i in range(3):
            adapter_copy(i, k).wait_send()

    @pl.loop(0, chunks)
    def _(i):
        for k in range(1, nc):
            rs_copy(i, k).wait_send()
            ag_copy(i, k).wait_send()


def fetch_adapters(factors, adapter_storage_slot, tile_adapter_index):
    per_holder = factors[0].shape[0]
    rows = lax.axis_size("row")
    me = lax.axis_index("row")
    adapters = jnp.arange(adapter_storage_slot.shape[0], dtype=jnp.int32)

    def slots_of(indices):
        pick = (indices[..., None] == adapters).astype(jnp.int32)
        return jnp.sum(pick * adapter_storage_slot, axis=-1)

    every = slots_of(lax.all_gather(tile_adapter_index, "row", axis=0, tiled=False))
    mine = slots_of(tile_adapter_index)
    residents = me * per_holder + jnp.arange(per_holder, dtype=jnp.int32)
    wanted = jnp.any(every[:, :, None] == residents, axis=1).astype(jnp.bfloat16)
    picked = [
        jnp.einsum("rf,fcd->rcd", wanted, f, preferred_element_type=jnp.float32).astype(jnp.bfloat16)
        for f in factors
    ]
    return picked, mine // per_holder


def per_device(
    nx,
    nz,
    hidden,
    up_weight,
    up_bias,
    down_weight,
    down_bias,
    query_key_value_weight,
    query_key_value_bias,
    block_norm_gain,
    block_norm_shift,
    following_norm_gain,
    following_norm_shift,
    up_down_factors,
    up_up_factors,
    query_key_value_down_factors,
    query_key_value_up_factors,
    adapter_storage_slot,
    tile_adapter_index,
    tile_token_rows,
):
    tok_rows, width = hidden.shape
    tile_len = tok_rows // tile_adapter_index.shape[0]
    nr, nc = nx * nz, lax.axis_size("col")
    piece = up_weight.shape[0]
    valid = (jnp.arange(tile_len, dtype=jnp.int32)[None, :] < tile_token_rows[:, None]).reshape(
        tok_rows, 1
    )
    (up_down, up_up, qkv_down, qkv_up), holder = fetch_adapters(
        [up_down_factors, up_up_factors, query_key_value_down_factors, query_key_value_up_factors],
        adapter_storage_slot,
        tile_adapter_index,
    )
    rank = up_down.shape[1]
    downs = jnp.stack([up_down, qkv_down], axis=1).reshape(nr, 2, rank, nr, piece)
    downs = downs.transpose(0, 1, 3, 2, 4)
    chunk = min(2 * tile_len, tok_rows)
    chunks = tok_rows // chunk
    hu, qc = up_weight.shape[1], query_key_value_weight.shape[1]
    dma = pltpu.SemaphoreType.DMA
    bf, f32 = jnp.bfloat16, jnp.float32
    anywhere = pl.BlockSpec(memory_space=pl.ANY)
    vmem = pl.BlockSpec(memory_space=pltpu.VMEM)
    return tuple(pl.pallas_call(
        functools.partial(fused_kernel, nx, nz, nc, tile_len, chunk),
        out_shape=[
            jax.ShapeDtypeStruct((tok_rows, width), bf),
            jax.ShapeDtypeStruct((tok_rows, qc), bf),
        ],
        in_specs=[pl.BlockSpec(memory_space=pltpu.SMEM)] + [anywhere] * 7 + [vmem] * 5,
        out_specs=[vmem, vmem],
        scratch_shapes=[
            pltpu.VMEM((nr, piece, hu), bf),
            pltpu.VMEM((nr, piece, hu), bf),
            pltpu.VMEM((nr, piece, qc), bf),
            pltpu.VMEM((nc, tok_rows, width), bf),
            pltpu.VMEM((nr, tok_rows, piece), bf),
            pltpu.VMEM((tok_rows, hu), bf),
            pltpu.VMEM((nc, tok_rows, width), bf),
            pltpu.VMEM((nc, tok_rows, width), bf),
            pltpu.VMEM((nc, tok_rows, width), bf),
            pltpu.VMEM(downs.shape, bf),
            pltpu.VMEM(up_up.shape, bf),
            pltpu.VMEM(qkv_up.shape, bf),
            pltpu.VMEM((chunk, max(hu, qc)), f32),
            pltpu.VMEM((chunk, width), f32),
            dma((7,)),
            dma((3, 2, nz)), dma((3, 2, nz)),
            dma((3, nx - 1, 2, 2 * nz)), dma((3, nx - 1, 2, 2 * nz)),
            dma((nc,)), dma((nc,)),
            dma((3, nr)), dma((3, nr)),
            dma((chunks, nc)), dma((chunks, nc)),
            dma((chunks, nc)), dma((chunks, nc)),
        ],
        compiler_params=pltpu.CompilerParams(
            collective_id=5, has_side_effects=True, vmem_limit_bytes=62 * 1024 * 1024
        ),
    )(
        holder, hidden, up_weight, down_weight.T, query_key_value_weight, downs, up_up, qkv_up,
        up_bias[None], down_bias[None], query_key_value_bias[None],
        jnp.concatenate(
            [block_norm_gain, block_norm_shift, following_norm_gain, following_norm_shift]
        ).reshape(4 * nc, 1, width),
        valid.astype(jnp.int32),
    ))


def solution(mesh):
    nx = max(mesh.shape["col"] // 2, 1)
    nz = mesh.shape["row"] // nx
    in_specs = (
        P("row", "col"),
        P("row", "col"),
        P("col"),
        P("col", "row"),
        P("col"),
        P("row", "col"),
        P("col"),
        P(),
        P(),
        P(),
        P(),
        P("row", None, None),
        P("row", None, "col"),
        P("row", None, None),
        P("row", None, "col"),
        P(),
        P("row"),
        P("row"),
    )
    return jax.shard_map(
        functools.partial(per_device, nx, nz),
        mesh=mesh,
        in_specs=in_specs,
        out_specs=(P("row", "col"), P("row", "col")),
        check_vma=False,
    )
```
